32 devices in a mesh: band: 8 (over y, x, core), member: 4 (over z).
Axes of the slice: x: 2, y: 2, z: 4, core: 2. Of those that a mesh axis runs over, the one named last changes fastest.
Arguments:
- state_field: bfloat16 [32, 1440, 128], P('band'), may hold values from -6 to 6
- observed_target: bfloat16 [32, 1440, 128], P('band'), may hold values from -6 to 6
- feature_jitter_amplitude: float32 [128], replicated, may hold values from 0.2 to 1
- leading_filter: bfloat16 [3, 3, 128, 128], replicated, may hold values from -0.1875 to 0.1875
- trailing_filter: bfloat16 [3, 3, 128, 128], replicated, may hold values from -0.1875 to 0.1875
- parallels_each_strip: int32 [8], replicated, may hold values from 1 to 4, 24 in all
- realization_random_keys: int32 [4], P('member'), may hold values from 0 to 999999
Outputs:
- crps_cells: float32 [32, 1440], P('band', 'member')
- mean_loss: float32 [], replicated
- grad_one: float32 [3, 3, 128, 128], replicated
- trailing_filter_derivative: float32 [3, 3, 128, 128], replicated
The draws below stay inside these ranges and needn't reach their ends.
Inputs may be any that keep to these rules, and one draw needn't show every extreme that they name: `parallels_each_strip`: each band holds 1 to 4 rows, together 24, and some band holds exactly 4.
All inputs are finite; a program needn't handle non-finite values.
Results may differ from the reference program's by a relative error of at most 0.00075.
The reference program's roundings to bfloat16 on the way count: a program that leaves them out, or rounds other values in their place, can miss the bound.
Values may be sent and summed in bfloat16 or wider, within the bound.
A program may use at most 128 MiB of HBM per device.

```python
import math
import jax
import jax.numpy as jnp
import numpy as np
from jax import lax

ROWS_MAX = 4
EASTWARD_POINTS = 1440
INNER_FEATURES = 128
GRID_ROWS = 721
MEMBERS = 4
ROWS = 32
ROWS_TOTAL = 24
N_BAND = 8
N_MEMBER = 4


def plant(drawn, rng, least, largest):
    spot = [jax.random.randint(jax.random.fold_in(rng, axis), (), 0, length) for axis, length in enumerate(drawn.shape)]
    longest = drawn.shape.index(max(drawn.shape))
    neighbour = spot[:longest] + [(spot[longest] + 1) % drawn.shape[longest]] + spot[longest + 1:]
    return drawn.at[tuple(spot)].set(least).at[tuple(neighbour)].set(largest)


def shard_levels(own_key, dims, cuts, least, largest):
    loudness, own = 1.0, jax.random.fold_in(own_key, 6)
    for position, blocks in cuts:
        draws = jnp.exp(jax.random.uniform(jax.random.fold_in(own, position), (blocks,), jnp.float32, least / len(cuts), largest / len(cuts)))
        loudness = loudness * jnp.repeat(draws, dims[position] // blocks).reshape([-1 if axis == position else 1 for axis in range(len(dims))])
    return loudness


def length_profile(number_of, total, bound, lean):
    weights = [(1 << 20) // math.isqrt(standing ** lean) + 1 for standing in range(2, number_of + 1)]
    rest, holding = total - bound - (number_of - 1), [1] * (number_of - 1)
    while rest > 0:
        free = [i for i in range(number_of - 1) if holding[i] < bound]
        pool, budget = sum([weights[i] for i in free]), rest
        for i in free:
            addition = min(bound - holding[i], max(1, budget * weights[i] // pool), rest)
            holding[i] = holding[i] + addition
            rest = rest - addition
    return np.array([bound] + holding)


def uneven(rng, amount, total, most, lean):
    if amount == 2:
        one = jax.random.randint(rng, (), max(1, total - most), min(most, total - 1) + 1)
        return jnp.stack([one, total - one])
    tallies = jnp.asarray(length_profile(amount, total, most, lean), jnp.int32)
    pairs = (amount - 1) // 2
    giver, taker = tallies[1:1 + 2 * pairs:2], tallies[2:2 + 2 * pairs:2]
    room = jnp.minimum(giver - 1, most - taker)
    moved = jax.random.randint(jax.random.fold_in(rng, 1), (pairs,), 0, 1 << 20) % (room + 1)
    tallies = tallies.at[1:1 + 2 * pairs:2].set(giver - moved).at[2:2 + 2 * pairs:2].set(taker + moved)
    return tallies[jax.random.permutation(jax.random.fold_in(rng, 2), amount)]


def noise(rng, shape, scale, reach, cuts=(), held_as=jnp.bfloat16):
    factor_of = shard_levels(rng, shape, cuts, -0.22, 0.18) if cuts else 1.0
    array = jax.random.normal(rng, shape, jnp.float32) * scale * factor_of
    return jnp.minimum(jnp.maximum(array, -reach), reach).astype(held_as)


def setup_inputs(seed: int = 0) -> dict:
    arg_keys = jax.random.split(jax.random.key(seed), 8)
    state_field = noise(arg_keys[0], (ROWS, EASTWARD_POINTS, INNER_FEATURES), 1.0, 6.0, ((0, 8),))
    observed_target = noise(arg_keys[1], (ROWS, EASTWARD_POINTS, INNER_FEATURES), 1.0, 6.0, ((0, 8),))
    feature_jitter_amplitude = jnp.clip(jnp.exp(jax.random.uniform(arg_keys[2], (INNER_FEATURES,), jnp.float32, math.log(0.2), math.log(1.0))), 0.2, 1.0)
    leading_filter = noise(arg_keys[3], (3, 3, INNER_FEATURES, INNER_FEATURES), (9 * INNER_FEATURES) ** -0.5, 0.1875)
    trailing_filter = noise(arg_keys[4], (3, 3, INNER_FEATURES, INNER_FEATURES), (9 * INNER_FEATURES) ** -0.5, 0.1875)
    parallels_each_strip = uneven(arg_keys[5], N_BAND, ROWS_TOTAL, ROWS_MAX, 2).astype(jnp.int32)
    realization_random_keys = plant(jax.random.randint(arg_keys[6], (MEMBERS,), 0, 1000000), jax.random.fold_in(arg_keys[6], 1), 0, 999999).astype(jnp.int32)
    return dict(state_field=state_field, observed_target=observed_target, feature_jitter_amplitude=feature_jitter_amplitude, leading_filter=leading_filter, trailing_filter=trailing_filter, parallels_each_strip=parallels_each_strip, realization_random_keys=realization_random_keys)


smooth_sq = 0.01

def cell_noise(seed_value, first_row, strip_depth, meridian_entries, channels):
    global_row = first_row.astype(jnp.int32) + jnp.arange(strip_depth, dtype=jnp.int32)
    col_ids = jnp.arange(meridian_entries, dtype=jnp.int32)
    chan_ids = jnp.arange(channels, dtype=jnp.int32)
    hashed = global_row[:, None, None] * 374761393 + col_ids[None, :, None] * 668265263
    hashed = hashed + chan_ids[None, None, :] * 1274126177 + seed_value.astype(jnp.int32) * 1103515245
    hashed = hashed ^ hashed >> 13
    hashed = hashed * 1274126177
    hashed = hashed ^ hashed >> 16
    return ((hashed & 65535).astype(jnp.float32) + 0.5) / 32768.0 - 1.0

def extend_band_rows(field, upper_row, lower_row, padded_parallels):
    zero_row = jnp.zeros_like(upper_row)
    padded = jnp.concatenate([upper_row[None], field, zero_row[None]], axis=0)
    padded = lax.dynamic_update_slice(padded, lower_row[None], (padded_parallels.astype(jnp.int32) + 1, jnp.int32(0), jnp.int32(0)))
    return jnp.concatenate([padded[:, -1:], padded, padded[:, :1]], axis=1)

def patch_rows(padded, strip_depth, meridian_entries):
    pieces = [padded[shift_row:shift_row + strip_depth, shift_col:shift_col + meridian_entries] for shift_row in range(3) for shift_col in range(3)]
    joined = jnp.concatenate(pieces, axis=2)
    return joined.reshape(strip_depth * meridian_entries, joined.shape[2])

def apply_taps(padded, kernel, strip_depth, meridian_entries):
    channels = kernel.shape[3]
    result = jnp.dot(patch_rows(padded, strip_depth, meridian_entries), kernel.reshape(9 * kernel.shape[2], channels), preferred_element_type=jnp.float32)
    return result.reshape(strip_depth, meridian_entries, channels)

def kernel_weight_gradient(padded, cotangent, strip_depth, meridian_entries):
    patches = patch_rows(padded, strip_depth, meridian_entries)
    flat = cotangent.reshape(strip_depth * meridian_entries, cotangent.shape[2])
    result = lax.dot_general(patches, flat, (((0,), (0,)), ((), ())), preferred_element_type=jnp.float32)
    return result.reshape(3, 3, flat.shape[1], flat.shape[1])

def reversed_filter(kernel):
    return jnp.transpose(kernel[::-1, ::-1], (0, 1, 3, 2))

def silu_slope(linear_response):
    sig = jax.nn.sigmoid(linear_response)
    return sig * (1.0 + linear_response * (1.0 - sig))

def unbiased_crps_parts(realization_prediction, observed_target, filter_coefficient, derivative_factor):
    realization_group = realization_prediction.shape[0]
    target = observed_target.astype(jnp.float32)
    crps_results = [realization_prediction[opening_realization_number].astype(jnp.float32) for opening_realization_number in range(realization_group)]
    skill_sum = jnp.zeros_like(target)
    spread_sum = jnp.zeros_like(target)
    slopes = []
    for opening_realization_number in range(realization_group):
        diff = crps_results[opening_realization_number] - target
        smooth = jnp.sqrt(diff * diff + smooth_sq)
        skill_sum = skill_sum + smooth
        slopes.append(diff / smooth / realization_group)
    pair_scale = 1.0 / (realization_group * (realization_group - 1))
    for opening_realization_number in range(realization_group):
        for index_b in range(opening_realization_number + 1, realization_group):
            diff = crps_results[opening_realization_number] - crps_results[index_b]
            smooth = jnp.sqrt(diff * diff + smooth_sq)
            spread_sum = spread_sum + smooth
            tilt = diff / smooth * pair_scale
            slopes[opening_realization_number] = slopes[opening_realization_number] - tilt
            slopes[index_b] = slopes[index_b] + tilt
    crps = skill_sum / realization_group - spread_sum * pair_scale
    crps_pointwise = lax.optimization_barrier(jnp.mean(crps, axis=-1)) * filter_coefficient[..., 0]
    grand_accumulation = jnp.sum(crps * filter_coefficient)
    filter_derivatives = (jnp.stack(slopes) * (filter_coefficient * derivative_factor)).astype(jnp.bfloat16)
    return (crps_pointwise, grand_accumulation, filter_derivatives)

def neighbours(field, parallels_each_strip):
    parallel_strips = field.shape[0]
    last_rows = field[jnp.arange(parallel_strips), parallels_each_strip - 1]
    zero_row = jnp.zeros_like(field[:1, 0])
    upper = jnp.concatenate([zero_row, last_rows[:-1]], axis=0)
    lower = jnp.concatenate([field[1:, 0], zero_row], axis=0)
    return (upper, lower)

def filter_all_strips(field, parallels_each_strip, kernel):
    upper, lower = neighbours(field, parallels_each_strip)
    strip_depth, meridian_entries = (field.shape[1], field.shape[2])

    def one_band(items):
        piece, upper_row, lower_row, padded_parallels = items
        return apply_taps(extend_band_rows(piece, upper_row, lower_row, padded_parallels), kernel, strip_depth, meridian_entries)
    return lax.map(one_band, (field, upper, lower, parallels_each_strip))

def derivative_all_strips(field, cotangent, parallels_each_strip):
    upper, lower = neighbours(field, parallels_each_strip)
    strip_depth, meridian_entries = (field.shape[1], field.shape[2])

    def one_band(items):
        piece, cot_piece, upper_row, lower_row, padded_parallels = items
        return kernel_weight_gradient(extend_band_rows(piece, upper_row, lower_row, padded_parallels), cot_piece, strip_depth, meridian_entries)
    return lax.optimization_barrier(jnp.sum(lax.map(one_band, (field, cotangent, upper, lower, parallels_each_strip)), axis=0))

def band_masks(parallels_each_strip, strip_depth):
    offsets = (jnp.cumsum(parallels_each_strip) - parallels_each_strip).astype(jnp.int32)
    row_ids = jnp.arange(strip_depth, dtype=jnp.int32)
    genuine_parallel_flags = (row_ids[None, :] < parallels_each_strip[:, None]).astype(jnp.float32)[:, :, None, None]
    return (offsets, row_ids, genuine_parallel_flags)

def evaluate_model(strip_split_field, parallels_each_strip, seed_value, feature_jitter_amplitude, leading_filter, trailing_filter):
    parallel_strips, strip_depth, meridian_entries, channels = strip_split_field.shape
    offsets, row_ids, genuine_parallel_flags = band_masks(parallels_each_strip, strip_depth)
    noise_field = jax.vmap(lambda start: cell_noise(seed_value, start, strip_depth, meridian_entries, channels))(offsets)
    perturbed_source = ((strip_split_field.astype(jnp.float32) + feature_jitter_amplitude * noise_field) * genuine_parallel_flags).astype(jnp.bfloat16)
    linear_response = filter_all_strips(perturbed_source, parallels_each_strip, leading_filter)
    inner_response = (jax.nn.silu(linear_response) * genuine_parallel_flags).astype(jnp.bfloat16)
    realization_prediction = ((perturbed_source.astype(jnp.float32) + filter_all_strips(inner_response, parallels_each_strip, trailing_filter)) * genuine_parallel_flags).astype(jnp.bfloat16)
    return (perturbed_source, linear_response, inner_response, realization_prediction)

def reference(state_field, observed_target, feature_jitter_amplitude, leading_filter, trailing_filter, parallels_each_strip, realization_random_keys):
    parallel_strips = N_BAND
    strip_depth = ROWS_MAX
    parallels_each_strip = parallels_each_strip.astype(jnp.int32)
    strip_split_field = state_field.reshape(parallel_strips, strip_depth, EASTWARD_POINTS, INNER_FEATURES)
    prediction_pile = []
    for single_realization in range(N_MEMBER):
        prediction_pile.append(evaluate_model(strip_split_field, parallels_each_strip, realization_random_keys[single_realization], feature_jitter_amplitude, leading_filter, trailing_filter)[3])
    realization_prediction = jnp.stack(prediction_pile).reshape(N_MEMBER, parallel_strips * strip_depth, EASTWARD_POINTS, INNER_FEATURES)
    offsets, row_ids, genuine_parallel_flags = band_masks(parallels_each_strip, strip_depth)
    global_row = (offsets[:, None] + row_ids[None, :]).astype(jnp.float32)
    latitude = jnp.pi * ((global_row + 0.5) / GRID_ROWS - 0.5)
    filter_coefficient = (jnp.cos(latitude)[:, :, None, None] * genuine_parallel_flags).reshape(parallel_strips * strip_depth, 1, 1)
    derivative_factor = 1.0 / math.sqrt(ROWS_TOTAL * EASTWARD_POINTS)
    crps_pointwise, grand_accumulation, filter_derivatives = unbiased_crps_parts(realization_prediction, observed_target, filter_coefficient, derivative_factor)
    grad_one = jnp.zeros((3, 3, INNER_FEATURES, INNER_FEATURES), jnp.float32)
    trailing_filter_derivative = jnp.zeros((3, 3, INNER_FEATURES, INNER_FEATURES), jnp.float32)
    for single_realization in range(N_MEMBER):
        perturbed_source, linear_response, inner_response, unused = evaluate_model(strip_split_field, parallels_each_strip, realization_random_keys[single_realization], feature_jitter_amplitude, leading_filter, trailing_filter)
        prediction_adjoint = filter_derivatives[single_realization].reshape(parallel_strips, strip_depth, EASTWARD_POINTS, INNER_FEATURES)
        inner_adjoint = filter_all_strips(prediction_adjoint, parallels_each_strip, reversed_filter(trailing_filter))
        pre_cot = (inner_adjoint * silu_slope(linear_response) * genuine_parallel_flags).astype(jnp.bfloat16)
        trailing_filter_derivative = trailing_filter_derivative + derivative_all_strips(inner_response, prediction_adjoint, parallels_each_strip)
        grad_one = grad_one + derivative_all_strips(perturbed_source, pre_cot, parallels_each_strip)
    mean_loss = grand_accumulation / (ROWS_TOTAL * EASTWARD_POINTS * INNER_FEATURES)
    return (crps_pointwise, mean_loss, grad_one, trailing_filter_derivative)
```

```python
import functools
import math

import jax
import jax.numpy as jnp
from jax import lax
from jax.experimental import pallas as pl
from jax.experimental.pallas import tpu as pltpu
from jax.sharding import PartitionSpec as P

GRID_ROWS = 721
REACH = 3
MARGIN = 4
MESH = pl.DeviceIdType.MESH

smooth_sq = 0.01


def exchange_kernel(bands, members, up_ref, down_ref, key_ref, *refs):
    (up1, up2, up3, down1, down2, down3, keys_ref, send_sems, recv_sems, ksend, krecv) = refs
    b = lax.axis_index("band")
    m = lax.axis_index("member")
    hops = (1, 2, 3)
    barrier = pltpu.get_barrier_semaphore()
    for hop in hops:
        for other in (lax.rem(b + hop, bands), lax.rem(b + bands - hop, bands)):
            pl.semaphore_signal(barrier, inc=1, device_id=(other, m), device_id_type=MESH)
    for step in range(1, members):
        other = lax.rem(m + step, members)
        pl.semaphore_signal(barrier, inc=1, device_id=(b, other), device_id_type=MESH)
    pl.semaphore_wait(barrier, 2 * len(hops) + members - 1)
    copies = []
    for step in range(1, members):
        other = lax.rem(m + step, members)
        copies.append(
            pltpu.make_async_remote_copy(
                src_ref=key_ref,
                dst_ref=keys_ref.at[m],
                send_sem=ksend.at[step],
                recv_sem=krecv.at[step],
                device_id=(b, other),
                device_id_type=MESH,
            )
        )
    plan = (
        (up_ref, (0, 4), up1, 1),
        (down_ref, (0, 4), down1, bands - 1),
        (up_ref, (1, 2), up2, 2),
        (down_ref, (1, 2), down2, bands - 2),
        (up_ref, (2, 1), up3, 3),
        (down_ref, (1, 1), down3, bands - 3),
    )
    for slot, (source, (first, count), target, hop) in enumerate(plan):
        copies.append(
            pltpu.make_async_remote_copy(
                src_ref=source.at[pl.ds(first, count)],
                dst_ref=target,
                send_sem=send_sems.at[slot],
                recv_sem=recv_sems.at[slot],
                device_id=(lax.rem(b + hop, bands), m),
                device_id_type=MESH,
            )
        )
    for copy in copies:
        copy.start()
    keys_ref[m] = key_ref[...]
    for copy in copies:
        copy.wait()


def exchange(up_pack, down_pack, key_tile, bands, members):
    width, channels = up_pack.shape[1:]
    rows = lambda count: jax.ShapeDtypeStruct((count, width, channels), jnp.bfloat16)
    vmem = pl.BlockSpec(memory_space=pltpu.VMEM)
    return pl.pallas_call(
        functools.partial(exchange_kernel, bands, members),
        out_shape=[rows(4), rows(2), rows(1), rows(4), rows(2), rows(1)]
        + [jax.ShapeDtypeStruct((members,) + key_tile.shape, jnp.int32)],
        in_specs=[vmem] * 3,
        out_specs=[vmem] * 7,
        scratch_shapes=[
            pltpu.SemaphoreType.DMA((6,)),
            pltpu.SemaphoreType.DMA((6,)),
            pltpu.SemaphoreType.DMA((members,)),
            pltpu.SemaphoreType.DMA((members,)),
        ],
        compiler_params=pltpu.CompilerParams(
            collective_id=0, has_side_effects=True, vmem_limit_bytes=16 * 2**20
        ),
    )(up_pack, down_pack, key_tile)


def sum_kernel(groups, grads_ref, loss_ref, out_ref, total_ref, *scratch):
    stages = len(groups)
    lands = scratch[:stages]
    tiles = scratch[stages : 2 * stages]
    acc, tile, bsend, brecv, tsend, trecv, gsend, grecv = scratch[2 * stages :]
    place = {"band": lax.axis_index("band"), "member": lax.axis_index("member")}

    def device_of(axis, stride, size, mine, other):
        moved = dict(place)
        moved[axis] = place[axis] + (other - mine) * stride
        return (moved["band"], moved["member"])

    mines = [lax.rem(place[axis] // stride, size) for axis, stride, size in groups]
    barrier = pltpu.get_barrier_semaphore()
    greeted = 0
    for (axis, stride, size), mine in zip(groups, mines):
        for step in range(1, size):
            other = lax.rem(mine + step, size)
            pl.semaphore_signal(
                barrier,
                inc=1,
                device_id=device_of(axis, stride, size, mine, other),
                device_id_type=MESH,
            )
            greeted += 1
    pl.semaphore_wait(barrier, greeted)

    span = grads_ref.shape[0]
    base = 0
    bases, spans, slot = [], [], 0
    source = grads_ref
    tile_source = loss_ref
    for stage, ((axis, stride, size), mine) in enumerate(zip(groups, mines)):
        part = span // size
        copies = []
        for step in range(1, size):
            other = lax.rem(mine + step, size)
            device = device_of(axis, stride, size, mine, other)
            copies.append(
                pltpu.make_async_remote_copy(
                    src_ref=source.at[pl.ds(pl.multiple_of(base + other * part, 8), part)],
                    dst_ref=lands[stage].at[step - 1],
                    send_sem=bsend.at[slot],
                    recv_sem=brecv.at[slot],
                    device_id=device,
                    device_id_type=MESH,
                )
            )
            copies.append(
                pltpu.make_async_remote_copy(
                    src_ref=tile_source,
                    dst_ref=tiles[stage].at[step - 1],
                    send_sem=tsend.at[slot],
                    recv_sem=trecv.at[slot],
                    device_id=device,
                    device_id_type=MESH,
                )
            )
            slot += 1
        for copy in copies:
            copy.start()
        for copy in copies:
            copy.wait()
        base = base + mine * part
        span = part
        rows = pl.ds(pl.multiple_of(base, 8), part)
        value = source[rows]
        small = tile_source[...]
        for step in range(1, size):
            value = value + lands[stage][step - 1]
            small = small + tiles[stage][step - 1]
        if stage == stages - 1:
            out_ref[rows] = value
            total_ref[...] = small
        else:
            acc[rows] = value
            tile[stage] = small
        source = acc
        tile_source = tile.at[stage] if stage < stages - 1 else None
        bases.append(base)
        spans.append(span)
    slot = 0
    for stage in reversed(range(stages)):
        axis, stride, size = groups[stage]
        mine = mines[stage]
        rows = pl.ds(pl.multiple_of(bases[stage], 8), spans[stage])
        copies = []
        for step in range(1, size):
            other = lax.rem(mine + step, size)
            copies.append(
                pltpu.make_async_remote_copy(
                    src_ref=out_ref.at[rows],
                    dst_ref=out_ref.at[rows],
                    send_sem=gsend.at[slot],
                    recv_sem=grecv.at[slot],
                    device_id=device_of(axis, stride, size, mine, other),
                    device_id_type=MESH,
                )
            )
            slot += 1
        for copy in copies:
            copy.start()
        for copy in copies:
            copy.wait()


def sum_everywhere(grads, loss_tile, bands, members):
    groups = (("band", 1, 2), ("band", 2, bands // 2), ("member", 1, members))
    rows, channels = grads.shape
    unit = 8 * bands * members
    padded = -(-rows // unit) * unit
    if padded != rows:
        grads = jnp.concatenate([grads, jnp.zeros((padded - rows, channels), jnp.float32)])
    vmem = pl.BlockSpec(memory_space=pltpu.VMEM)
    lands, tiles, span, slots = [], [], padded, 0
    for _, _, size in groups:
        span //= size
        lands.append(pltpu.VMEM((size - 1, span, channels), jnp.float32))
        tiles.append(pltpu.VMEM((size - 1, 8, channels), jnp.float32))
        slots += size - 1
    out, total = pl.pallas_call(
        functools.partial(sum_kernel, groups),
        out_shape=[
            jax.ShapeDtypeStruct((padded, channels), jnp.float32),
            jax.ShapeDtypeStruct((8, channels), jnp.float32),
        ],
        in_specs=[vmem] * 2,
        out_specs=[vmem] * 2,
        scratch_shapes=lands
        + tiles
        + [
            pltpu.VMEM((padded, channels), jnp.float32),
            pltpu.VMEM((len(groups), 8, channels), jnp.float32),
        ]
        + [pltpu.SemaphoreType.DMA((slots,))] * 6,
        compiler_params=pltpu.CompilerParams(
            collective_id=1, has_side_effects=True, vmem_limit_bytes=24 * 2**20
        ),
    )(grads, loss_tile)
    return out[:rows], total


def noise_at(key, rows, cols, channels):
    chan = jnp.arange(channels, dtype=jnp.int32)
    hashed = rows[:, None, None] * 374761393 + cols[None, :, None] * 668265263
    hashed = hashed + chan[None, None, :] * 1274126177 + key * 1103515245
    hashed = hashed ^ hashed >> 13
    hashed = hashed * 1274126177
    hashed = hashed ^ hashed >> 16
    return ((hashed & 65535).astype(jnp.float32) + 0.5) / 32768.0 - 1.0


def gathered_rows(state_field, observed_target, parallels_each_strip, key, bands, members):
    strip, cells, channels = state_field.shape
    b = lax.axis_index("band")
    m = lax.axis_index("member")
    n = parallels_each_strip[b]
    quarter = cells // members
    width = quarter + 2 * MARGIN

    def window(field):
        wrapped = jnp.concatenate([field[:, -MARGIN:], field, field[:, :MARGIN]], axis=1)
        return lax.dynamic_slice_in_dim(wrapped, m * quarter, width, 1)

    own_s = window(state_field)
    own_t = window(observed_target)
    pick = lambda field, row: lax.dynamic_index_in_dim(
        field, jnp.clip(row, 0, strip - 1), 0, keepdims=False
    )
    up_pack = jnp.stack([pick(own_s, n - 3), pick(own_s, n - 2), pick(own_s, n - 1), pick(own_t, n - 1)])
    down_pack = jnp.stack([own_t[0], own_s[0], own_s[1], own_s[2]])
    key_tile = jnp.broadcast_to(key, (8, 128)).astype(jnp.int32)
    up1, up2, up3, down1, down2, down3, keys = exchange(
        up_pack, down_pack, key_tile, bands, members
    )
    states = jnp.concatenate([up3, up2, up1[:3], own_s, down1[1:], down2, down3])
    targets = jnp.concatenate([up1[3:], own_t, down1[:1]])
    near = lambda hop: parallels_each_strip[lax.rem(b + hop + bands, bands)]
    before1, before2, after1, after2 = near(-1), near(-2), near(1), near(2)
    slots = jnp.arange(strip + 2 * REACH, dtype=jnp.int32)
    above = REACH - slots
    below = slots - REACH - n + 1
    above_at = jnp.where(
        above <= before1, 6 - above, jnp.where(above - before1 <= before2, 3 - above + before1, 0)
    )
    last = 6 + strip - 1
    below_at = jnp.where(
        below <= after1,
        last + below,
        jnp.where(below - after1 <= after2, last + 3 + below - after1, last + 6),
    )
    state_at = jnp.where(above > 0, above_at, jnp.where(below <= 0, 6 + slots - REACH, below_at))
    inner = slots[2:-2] - 2
    target_at = jnp.where(inner <= n, inner, strip + 1)
    return states, targets, state_at, target_at, keys[:, 0, 0]


def patch_rows(padded, rows, cols):
    members = padded.shape[0]
    pieces = [padded[:, r : r + rows, c : c + cols] for r in range(3) for c in range(3)]
    joined = jnp.concatenate(pieces, axis=3)
    return joined.reshape(members * rows * cols, joined.shape[3])


def apply_taps(padded, kernel):
    members, rows, cols = padded.shape[0], padded.shape[1] - 2, padded.shape[2] - 2
    result = jnp.dot(
        patch_rows(padded, rows, cols),
        kernel.reshape(-1, kernel.shape[3]),
        preferred_element_type=jnp.float32,
    )
    return result.reshape(members, rows, cols, kernel.shape[3])


def tap_gradient(padded, cot):
    members, rows, cols, channels = cot.shape
    return lax.dot_general(
        patch_rows(padded, rows, cols),
        cot.reshape(-1, channels),
        (((0,), (0,)), ((), ())),
        preferred_element_type=jnp.float32,
    )


def silu_slope(response):
    sig = jax.nn.sigmoid(response)
    return sig * (1.0 + response * (1.0 - sig))


def crps_parts(forecast, target):
    members = forecast.shape[0]
    cells = [forecast[i].astype(jnp.float32) for i in range(members)]
    skill, spread, slopes = 0.0, 0.0, []
    for i in range(members):
        diff = cells[i] - target
        smooth = jnp.sqrt(diff * diff + smooth_sq)
        skill = skill + smooth
        slopes.append(diff / smooth / members)
    pair_scale = 1.0 / (members * (members - 1))
    for i in range(members):
        for j in range(i + 1, members):
            diff = cells[i] - cells[j]
            smooth = jnp.sqrt(diff * diff + smooth_sq)
            spread = spread + smooth
            tilt = diff / smooth * pair_scale
            slopes[i] = slopes[i] - tilt
            slopes[j] = slopes[j] + tilt
    return skill / members - spread * pair_scale, jnp.stack(slopes)


def body(state_field, observed_target, amplitude, leading, trailing, parallels_each_strip, key):
    strip, cells, channels = state_field.shape
    bands = lax.axis_size("band")
    members = lax.axis_size("member")
    b = lax.axis_index("band")
    m = lax.axis_index("member")
    quarter = cells // members
    rows_total = 3 * strip * bands // 4
    n = parallels_each_strip[b]
    offset = jnp.sum(
        jnp.where(jnp.arange(bands, dtype=jnp.int32) < b, parallels_each_strip, 0)
    )
    states, targets, state_at, target_at, keys = gathered_rows(
        state_field, observed_target, parallels_each_strip, key, bands, members
    )
    take = lambda field, at: jnp.stack(
        [lax.dynamic_index_in_dim(field, at[k], 0, keepdims=False) for k in range(at.shape[0])]
    )
    state = take(states, state_at)
    target = take(targets, target_at)
    grid = offset - REACH + jnp.arange(strip + 2 * REACH, dtype=jnp.int32)
    valid = ((grid >= 0) & (grid < rows_total)).astype(jnp.float32)[:, None, None]
    owned = (jnp.arange(strip) < n).astype(jnp.float32)[:, None, None]
    columns = lax.rem(
        m * quarter + cells - MARGIN + jnp.arange(quarter + 2 * MARGIN, dtype=jnp.int32), cells
    )
    weight = (
        jnp.cos(jnp.pi * ((grid.astype(jnp.float32) + 0.5) / GRID_ROWS - 0.5))[:, None, None] * valid
    )
    derivative_factor = 1.0 / math.sqrt(rows_total * cells)
    noise = jnp.stack([noise_at(keys[i], grid, columns, channels) for i in range(members)])
    inputs = ((state.astype(jnp.float32) + amplitude * noise) * valid).astype(jnp.bfloat16)
    pre_act = apply_taps(inputs, leading)
    hidden = (jax.nn.silu(pre_act) * valid[1:-1]).astype(jnp.bfloat16)
    forecast = (
        (inputs[:, 2:-2, 2:-2].astype(jnp.float32) + apply_taps(hidden, trailing)) * valid[2:-2]
    ).astype(jnp.bfloat16)
    crps, slopes = crps_parts(forecast, target[:, 2:-2].astype(jnp.float32))
    cot = (slopes * (weight[2:-2] * derivative_factor)).astype(jnp.bfloat16)
    own_crps = crps[1:-1, 2:-2]
    own_weight = weight[3:-3] * owned
    crps_cells = jnp.mean(own_crps, axis=-1) * own_weight[..., 0]
    loss = jnp.sum(own_crps * own_weight)
    reversed_filter = jnp.transpose(trailing[::-1, ::-1], (0, 1, 3, 2))
    hidden_cot = apply_taps(cot[:, :, 1:-1], reversed_filter)
    pre_cot = (hidden_cot * silu_slope(pre_act[:, 2:-2, 3:-3]) * owned).astype(jnp.bfloat16)
    own_cot = cot[:, 1:-1, 2:-2] * owned.astype(jnp.bfloat16)
    grad_two = tap_gradient(hidden[:, 1:-1, 2:-2], own_cot)
    grad_one = tap_gradient(inputs[:, 2:-2, 3:-3], pre_cot)
    loss_tile = jnp.broadcast_to(loss, (8, 128))
    summed, total = sum_everywhere(
        jnp.concatenate([grad_one, grad_two]), loss_tile, bands, members
    )
    half = summed.shape[0] // 2
    return (
        crps_cells,
        total[0, 0] / (rows_total * cells * channels),
        summed[:half].reshape(leading.shape),
        summed[half:].reshape(trailing.shape),
    )


def solution(mesh):
    in_specs = (P("band", None, None), P("band", None, None), P(), P(), P(), P(), P("member"))
    out_specs = (P("band", "member"), P(), P(), P())
    return jax.shard_map(body, mesh=mesh, in_specs=in_specs, out_specs=out_specs, check_vma=False)
```

```python
import functools
import math

import jax
import jax.numpy as jnp
from jax import lax
from jax.experimental import pallas as pl
from jax.experimental.pallas import tpu as pltpu
from jax.sharding import PartitionSpec as P

GRID_ROWS = 721
REACH = 3
MARGIN = 4
MESH = pl.DeviceIdType.MESH

smooth_sq = 0.01


def exchange_kernel(bands, members, up_ref, down_ref, key_ref, *refs):
    (up1, up2, up3, down1, down2, down3, keys_ref, send_sems, recv_sems, ksend, krecv) = refs
    b = lax.axis_index("band")
    m = lax.axis_index("member")
    hops = (1, 2, 3)
    barrier = pltpu.get_barrier_semaphore()
    for hop in hops:
        for other in (lax.rem(b + hop, bands), lax.rem(b + bands - hop, bands)):
            pl.semaphore_signal(barrier, inc=1, device_id=(other, m), device_id_type=MESH)
    for step in range(1, members):
        other = lax.rem(m + step, members)
        pl.semaphore_signal(barrier, inc=1, device_id=(b, other), device_id_type=MESH)
    pl.semaphore_wait(barrier, 2 * len(hops) + members - 1)
    copies = []
    for step in range(1, members):
        other = lax.rem(m + step, members)
        copies.append(
            pltpu.make_async_remote_copy(
                src_ref=key_ref,
                dst_ref=keys_ref.at[m],
                send_sem=ksend.at[step],
                recv_sem=krecv.at[step],
                device_id=(b, other),
                device_id_type=MESH,
            )
        )
    plan = (
        (up_ref, (0, 4), up1, 1),
        (down_ref, (0, 4), down1, bands - 1),
        (up_ref, (1, 2), up2, 2),
        (down_ref, (1, 2), down2, bands - 2),
        (up_ref, (2, 1), up3, 3),
        (down_ref, (1, 1), down3, bands - 3),
    )
    for slot, (source, (first, count), target, hop) in enumerate(plan):
        copies.append(
            pltpu.make_async_remote_copy(
                src_ref=source.at[pl.ds(first, count)],
                dst_ref=target,
                send_sem=send_sems.at[slot],
                recv_sem=recv_sems.at[slot],
                device_id=(lax.rem(b + hop, bands), m),
                device_id_type=MESH,
            )
        )
    for copy in copies:
        copy.start()
    keys_ref[m] = key_ref[...]
    for copy in copies:
        copy.wait()


def exchange(up_pack, down_pack, key_tile, bands, members):
    width, channels = up_pack.shape[1:]
    rows = lambda count: jax.ShapeDtypeStruct((count, width, channels), jnp.bfloat16)
    vmem = pl.BlockSpec(memory_space=pltpu.VMEM)
    return pl.pallas_call(
        functools.partial(exchange_kernel, bands, members),
        out_shape=[rows(4), rows(2), rows(1), rows(4), rows(2), rows(1)]
        + [jax.ShapeDtypeStruct((members,) + key_tile.shape, jnp.int32)],
        in_specs=[vmem] * 3,
        out_specs=[vmem] * 7,
        scratch_shapes=[
            pltpu.SemaphoreType.DMA((6,)),
            pltpu.SemaphoreType.DMA((6,)),
            pltpu.SemaphoreType.DMA((members,)),
            pltpu.SemaphoreType.DMA((members,)),
        ],
        compiler_params=pltpu.CompilerParams(
            collective_id=0, has_side_effects=True, vmem_limit_bytes=16 * 2**20
        ),
    )(up_pack, down_pack, key_tile)


def sum_kernel(groups, grads_ref, loss_ref, out_ref, total_ref, *scratch):
    stages = len(groups)
    lands = scratch[:stages]
    tiles = scratch[stages : 2 * stages]
    acc, tile, bsend, brecv, tsend, trecv, gsend, grecv = scratch[2 * stages :]
    place = {"band": lax.axis_index("band"), "member": lax.axis_index("member")}

    def device_of(axis, stride, size, mine, other):
        moved = dict(place)
        moved[axis] = place[axis] + (other - mine) * stride
        return (moved["band"], moved["member"])

    mines = [lax.rem(place[axis] // stride, size) for axis, stride, size in groups]
    barrier = pltpu.get_barrier_semaphore()
    greeted = 0
    for (axis, stride, size), mine in zip(groups, mines):
        for step in range(1, size):
            other = lax.rem(mine + step, size)
            pl.semaphore_signal(
                barrier,
                inc=1,
                device_id=device_of(axis, stride, size, mine, other),
                device_id_type=MESH,
            )
            greeted += 1
    pl.semaphore_wait(barrier, greeted)

    span = grads_ref.shape[0]
    base = 0
    bases, spans, slot = [], [], 0
    source = grads_ref
    tile_source = loss_ref
    for stage, ((axis, stride, size), mine) in enumerate(zip(groups, mines)):
        part = span // size
        copies = []
        for step in range(1, size):
            other = lax.rem(mine + step, size)
            device = device_of(axis, stride, size, mine, other)
            copies.append(
                pltpu.make_async_remote_copy(
                    src_ref=source.at[pl.ds(pl.multiple_of(base + other * part, 8), part)],
                    dst_ref=lands[stage].at[step - 1],
                    send_sem=bsend.at[slot],
                    recv_sem=brecv.at[slot],
                    device_id=device,
                    device_id_type=MESH,
                )
            )
            copies.append(
                pltpu.make_async_remote_copy(
                    src_ref=tile_source,
                    dst_ref=tiles[stage].at[step - 1],
                    send_sem=tsend.at[slot],
                    recv_sem=trecv.at[slot],
                    device_id=device,
                    device_id_type=MESH,
                )
            )
            slot += 1
        for copy in copies:
            copy.start()
        for copy in copies:
            copy.wait()
        base = base + mine * part
        span = part
        rows = pl.ds(pl.multiple_of(base, 8), part)
        value = source[rows]
        small = tile_source[...]
        for step in range(1, size):
            value = value + lands[stage][step - 1]
            small = small + tiles[stage][step - 1]
        if stage == stages - 1:
            out_ref[rows] = value
            total_ref[...] = small
        else:
            acc[rows] = value
            tile[stage] = small
        source = acc
        tile_source = tile.at[stage] if stage < stages - 1 else None
        bases.append(base)
        spans.append(span)
    slot = 0
    for stage in reversed(range(stages)):
        axis, stride, size = groups[stage]
        mine = mines[stage]
        rows = pl.ds(pl.multiple_of(bases[stage], 8), spans[stage])
        copies = []
        for step in range(1, size):
            other = lax.rem(mine + step, size)
            copies.append(
                pltpu.make_async_remote_copy(
                    src_ref=out_ref.at[rows],
                    dst_ref=out_ref.at[rows],
                    send_sem=gsend.at[slot],
                    recv_sem=grecv.at[slot],
                    device_id=device_of(axis, stride, size, mine, other),
                    device_id_type=MESH,
                )
            )
            slot += 1
        for copy in copies:
            copy.start()
        for copy in copies:
            copy.wait()


def sum_everywhere(grads, loss_tile, bands, members):
    groups = (("band", 1, 2), ("band", 2, bands // 2), ("member", 1, members))
    rows, channels = grads.shape
    unit = 8 * bands * members
    padded = -(-rows // unit) * unit
    if padded != rows:
        grads = jnp.concatenate([grads, jnp.zeros((padded - rows, channels), jnp.float32)])
    vmem = pl.BlockSpec(memory_space=pltpu.VMEM)
    lands, tiles, span, slots = [], [], padded, 0
    for _, _, size in groups:
        span //= size
        lands.append(pltpu.VMEM((size - 1, span, channels), jnp.float32))
        tiles.append(pltpu.VMEM((size - 1, 8, channels), jnp.float32))
        slots += size - 1
    out, total = pl.pallas_call(
        functools.partial(sum_kernel, groups),
        out_shape=[
            jax.ShapeDtypeStruct((padded, channels), jnp.float32),
            jax.ShapeDtypeStruct((8, channels), jnp.float32),
        ],
        in_specs=[vmem] * 2,
        out_specs=[vmem] * 2,
        scratch_shapes=lands
        + tiles
        + [
            pltpu.VMEM((padded, channels), jnp.float32),
            pltpu.VMEM((len(groups), 8, channels), jnp.float32),
        ]
        + [pltpu.SemaphoreType.DMA((slots,))] * 6,
        compiler_params=pltpu.CompilerParams(
            collective_id=1, has_side_effects=True, vmem_limit_bytes=24 * 2**20
        ),
    )(grads, loss_tile)
    return out[:rows], total


def gathered_rows(state_field, observed_target, parallels_each_strip, key, bands, members):
    strip, cells, channels = state_field.shape
    b = lax.axis_index("band")
    m = lax.axis_index("member")
    n = parallels_each_strip[b]
    quarter = cells // members
    width = quarter + 2 * MARGIN

    def window(field):
        cut = lambda at, count: lax.dynamic_slice_in_dim(field, lax.rem(at, cells), count, 1)
        start = m * quarter
        return jnp.concatenate(
            [cut(start + cells - MARGIN, MARGIN), cut(start, quarter), cut(start + quarter, MARGIN)],
            axis=1,
        )

    own_s = window(state_field)
    own_t = window(observed_target)
    pick = lambda field, row: lax.dynamic_index_in_dim(
        field, jnp.clip(row, 0, strip - 1), 0, keepdims=False
    )
    up_pack = jnp.stack([pick(own_s, n - 3), pick(own_s, n - 2), pick(own_s, n - 1), pick(own_t, n - 1)])
    down_pack = jnp.stack([own_t[0], own_s[0], own_s[1], own_s[2]])
    key_tile = jnp.broadcast_to(key, (8, 128)).astype(jnp.int32)
    up1, up2, up3, down1, down2, down3, keys = exchange(
        up_pack, down_pack, key_tile, bands, members
    )
    states = jnp.concatenate([up3, up2, up1[:3], own_s, down1[1:], down2, down3])
    targets = jnp.concatenate([up1[3:], own_t, down1[:1]])
    near = lambda hop: parallels_each_strip[lax.rem(b + hop + bands, bands)]
    before1, before2, after1, after2 = near(-1), near(-2), near(1), near(2)
    slots = jnp.arange(strip + 2 * REACH, dtype=jnp.int32)
    above = REACH - slots
    below = slots - REACH - n + 1
    above_at = jnp.where(
        above <= before1, 6 - above, jnp.where(above - before1 <= before2, 3 - above + before1, 0)
    )
    last = 6 + strip - 1
    below_at = jnp.where(
        below <= after1,
        last + below,
        jnp.where(below - after1 <= after2, last + 3 + below - after1, last + 6),
    )
    state_at = jnp.where(above > 0, above_at, jnp.where(below <= 0, 6 + slots - REACH, below_at))
    inner = slots[2:-2] - 2
    target_at = jnp.where(inner <= n, inner, strip + 1)
    return states, targets, state_at, target_at, keys[:, 0, 0]


def step_kernel(
    strip, members, cells, ints_ref, floats_ref, states_ref, targets_ref, amplitude_ref,
    first_ref, second_ref, back_ref, grads_ref, means_ref,
    in_taps, hid_taps, cot_taps, slope_ref, forecast_ref, own_cot, pre_cot,
):
    rows = strip + 2 * REACH
    width, channels = states_ref.shape[1:]
    row0 = ints_ref[2 * rows - 4]
    col0 = ints_ref[2 * rows - 3]
    bf16, f32 = jnp.bfloat16, jnp.float32
    place = lax.broadcasted_iota(jnp.int32, (width, channels), 0)
    chan = lax.broadcasted_iota(jnp.int32, (width, channels), 1)
    inside = ((place >= MARGIN) & (place < width - MARGIN)).astype(f32)

    def put_taps(ref, m, k, value):
        ref[m, k, :, 0:channels] = pltpu.roll(value, 1, 0).astype(bf16)
        ref[m, k, :, channels : 2 * channels] = value.astype(bf16)
        ref[m, k, :, 2 * channels : 3 * channels] = pltpu.roll(value, width - 1, 0).astype(bf16)

    def conv(ref, m, k, kernel_ref):
        patches = jnp.concatenate([ref[m, k], ref[m, k + 1], ref[m, k + 2]], axis=1)
        return jnp.dot(patches, kernel_ref[...], preferred_element_type=f32)

    col = col0 + place
    col = jnp.where(col >= cells, col - cells, col)
    base = col * 668265263 + chan * 1274126177
    amplitude = amplitude_ref[...]

    def make_inputs(step, carry):
        m, k = step // rows, step % rows
        key = ints_ref[2 * rows - 2 + m]
        hashed = base + ((row0 + k) * 374761393 + key * 1103515245)
        hashed = hashed ^ hashed >> 13
        hashed = hashed * 1274126177
        hashed = hashed ^ hashed >> 16
        noise = ((hashed & 65535).astype(f32) + 0.5) / 32768.0 - 1.0
        state = states_ref[ints_ref[k]].astype(f32)
        value = (state + amplitude * noise) * floats_ref[k]
        put_taps(in_taps, m, k, value.astype(bf16).astype(f32))
        return carry

    lax.fori_loop(0, members * rows, make_inputs, 0)

    def make_hidden(step, carry):
        m, k = step // (rows - 2), step % (rows - 2)
        pre = conv(in_taps, m, k, first_ref)
        sig = jax.nn.sigmoid(pre)
        hidden = (pre * sig * floats_ref[k + 1]).astype(bf16)
        slope_ref[m, k] = sig * (1.0 + pre * (1.0 - sig))
        put_taps(hid_taps, m, k, hidden.astype(f32))
        return carry

    lax.fori_loop(0, members * (rows - 2), make_hidden, 0)

    def make_forecast(step, carry):
        m, k = step // (rows - 4), step % (rows - 4)
        source = in_taps[m, k + 2, :, channels : 2 * channels].astype(f32)
        value = (source + conv(hid_taps, m, k, second_ref)) * floats_ref[k + 2]
        forecast_ref[m, k] = value.astype(bf16)
        return carry

    lax.fori_loop(0, members * (rows - 4), make_forecast, 0)

    pair_scale = 1.0 / (members * (members - 1))

    def make_score(k, carry):
        weight = floats_ref[rows + k]
        target_row = ints_ref[rows + k]
        for low in range(0, width, 16):
            part = slice(low, low + 16)
            truth = targets_ref[target_row, part].astype(f32)
            field = [forecast_ref[i, k, part].astype(f32) for i in range(members)]
            skill, spread, slopes = 0.0, 0.0, []
            for i in range(members):
                diff = field[i] - truth
                square = diff * diff + smooth_sq
                inverse = lax.rsqrt(square)
                skill = skill + square * inverse
                slopes.append(diff * inverse * (1.0 / members))
            for i in range(members):
                for j in range(i + 1, members):
                    diff = field[i] - field[j]
                    square = diff * diff + smooth_sq
                    inverse = lax.rsqrt(square)
                    spread = spread + square * inverse
                    tilt = diff * inverse * pair_scale
                    slopes[i] = slopes[i] - tilt
                    slopes[j] = slopes[j] + tilt
            crps = skill * (1.0 / members) - spread * pair_scale
            means_ref[k, part, :] = jnp.sum(crps, axis=1, keepdims=True) * (1.0 / channels)
            for i in range(members):
                forecast_ref[i, k, part] = (slopes[i] * weight).astype(bf16)
        return carry

    lax.fori_loop(0, rows - 4, make_score, 0)

    def spread_cot(step, carry):
        m, k = step // (rows - 4), step % (rows - 4)
        put_taps(cot_taps, m, k, forecast_ref[m, k].astype(f32))
        return carry

    lax.fori_loop(0, members * (rows - 4), spread_cot, 0)

    def make_pre_cot(step, carry):
        m, k = step // strip, step % strip
        mask = inside * floats_ref[2 * rows - 4 + k]
        own_cot[m, k] = (forecast_ref[m, k + 1].astype(f32) * mask).astype(bf16)
        value = conv(cot_taps, m, k, back_ref) * slope_ref[m, k + 2] * mask
        pre_cot[m, k] = value.astype(bf16)
        return carry

    lax.fori_loop(0, members * strip, make_pre_cot, 0)

    def gradient(cot_ref, taps_ref, first, out_row):
        pixels = strip * width
        for r in range(3):
            total = None
            for m in range(members):
                term = lax.dot_general(
                    cot_ref[m].reshape(pixels, channels),
                    taps_ref[m, first + r : first + r + strip].reshape(pixels, 3 * channels),
                    (((0,), (0,)), ((), ())),
                    preferred_element_type=f32,
                )
                total = term if total is None else total + term
            low = out_row + r * 3 * channels
            grads_ref[low : low + 3 * channels] = total.T

    gradient(pre_cot, in_taps, REACH - 1, 0)
    gradient(own_cot, hid_taps, REACH - 2, 9 * channels)


def run_step(ints, floats, states, targets, amplitude, first, second, back, strip, members, cells):
    rows = strip + 2 * REACH
    width, channels = states.shape[1:]
    vmem = pl.BlockSpec(memory_space=pltpu.VMEM)
    smem = pl.BlockSpec(memory_space=pltpu.SMEM)
    wide = lambda count: pltpu.VMEM((members, count, width, 3 * channels), jnp.bfloat16)
    thin = lambda count, dtype: pltpu.VMEM((members, count, width, channels), dtype)
    return pl.pallas_call(
        functools.partial(step_kernel, strip, members, cells),
        out_shape=[
            jax.ShapeDtypeStruct((18 * channels, channels), jnp.float32),
            jax.ShapeDtypeStruct((rows - 4, width, 1), jnp.float32),
        ],
        in_specs=[smem] * 2 + [vmem] * 6,
        out_specs=[vmem] * 2,
        scratch_shapes=[
            wide(rows),
            wide(rows - 2),
            wide(rows - 4),
            thin(rows - 2, jnp.float32),
            thin(rows - 4, jnp.bfloat16),
            thin(strip, jnp.bfloat16),
            thin(strip, jnp.bfloat16),
        ],
        compiler_params=pltpu.CompilerParams(vmem_limit_bytes=58 * 2**20),
    )(ints, floats, states, targets, amplitude, first, second, back)


def body(state_field, observed_target, amplitude, leading, trailing, parallels_each_strip, key):
    strip, cells, channels = state_field.shape
    bands = lax.axis_size("band")
    members = lax.axis_size("member")
    b = lax.axis_index("band")
    m = lax.axis_index("member")
    quarter = cells // members
    rows_total = 3 * strip * bands // 4
    n = parallels_each_strip[b]
    offset = jnp.sum(
        jnp.where(jnp.arange(bands, dtype=jnp.int32) < b, parallels_each_strip, 0)
    )
    states, targets, state_at, target_at, keys = gathered_rows(
        state_field, observed_target, parallels_each_strip, key, bands, members
    )
    grid = offset - REACH + jnp.arange(strip + 2 * REACH, dtype=jnp.int32)
    valid = ((grid >= 0) & (grid < rows_total)).astype(jnp.float32)
    owned = (jnp.arange(strip) < n).astype(jnp.float32)
    weight = jnp.cos(jnp.pi * ((grid.astype(jnp.float32) + 0.5) / GRID_ROWS - 0.5)) * valid
    derivative_factor = 1.0 / math.sqrt(rows_total * cells)
    col0 = lax.rem(m * quarter + cells - MARGIN, cells)
    ints = jnp.concatenate(
        [state_at, target_at, jnp.stack([offset - REACH, col0]), keys]
    ).astype(jnp.int32)
    floats = jnp.concatenate([valid, weight[2:-2] * derivative_factor, owned])
    reversed_filter = jnp.transpose(trailing[::-1, ::-1], (0, 1, 3, 2))
    flat = lambda kernel: kernel.reshape(9 * channels, channels)
    grads, means = run_step(
        ints, floats, states, targets, amplitude.reshape(1, channels),
        flat(leading), flat(trailing), flat(reversed_filter), strip, members, cells,
    )
    own_weight = weight[3:-3] * owned
    crps_cells = means[1:-1, MARGIN:-MARGIN, 0] * own_weight[:, None]
    loss_tile = jnp.broadcast_to(jnp.sum(crps_cells) * channels, (8, 128))
    summed, total = sum_everywhere(grads, loss_tile, bands, members)
    half = summed.shape[0] // 2
    return (
        crps_cells,
        total[0, 0] / (rows_total * cells * channels),
        summed[:half].reshape(leading.shape),
        summed[half:].reshape(trailing.shape),
    )


def solution(mesh):
    in_specs = (P("band", None, None), P("band", None, None), P(), P(), P(), P(), P("member"))
    out_specs = (P("band", "member"), P(), P(), P())
    return jax.shard_map(body, mesh=mesh, in_specs=in_specs, out_specs=out_specs, check_vma=False)
```
